256 devices in a mesh: step: 2 (over core), head: 8 (over z), blk: 16 (over y, x).
Axes of the slice: x: 4, y: 4, z: 8, core: 2. Of those that a mesh axis runs over, the one named last changes fastest.
Arguments:
- states: float32 [2, 2048, 3072], P('step', ('head', 'blk')), may hold values from -6 to 6
- start: float32 [2048, 3072], P(('head', 'blk')), may hold values from -6 to 6
- w_qkv: bfloat16 [3072, 3, 3072], P('blk', None, 'head'), may hold values from -0.109375 to 0.109375
- w_out: bfloat16 [3072, 3072], P(('head', 'blk')), may hold values from -0.109375 to 0.109375
- q_gain: float32 [64], replicated, may hold values from 1.5 to 5
- k_gain: float32 [64], replicated, may hold values from 1.5 to 5
- mod_table: float32 [50, 9216], replicated, may hold values from -3 to 3
- step_index: int32 [2], P('step'), may hold values from 0 to 49
- coef_table: float32 [50], replicated, may hold values from 0.1 to 1
- coef_index: int32 [2], P('step'), may hold values from 0 to 49
Outputs:
- new_states: float32 [2, 2048, 3072], P('step', ('head', 'blk'))
The draws below stay inside these ranges and needn't reach their ends.
All inputs are finite; a program needn't handle non-finite values.
Results may differ from the reference program's by a relative error of at most 0.008.
Values may be sent and summed in bfloat16 or wider, within the bound.
No kernel may reach another device: no remote copies, remote signals or barrier semaphores. Data moves between devices by JAX's collectives and lax.ppermute only.
A program may use at most 128 MiB of HBM per device.

```python
import math
import jax
import jax.numpy as jnp
from jax import lax

D = 3072
H = 48
HD = 64
TABLE = 50
STEPS = 2
L = 2048


def draw_q_gain(key, part):
    key = jax.random.fold_in(key, 11)
    return jax.random.uniform(key, (HD,), jnp.float32, 1.5, 2.5)


def draw_k_gain(key, part):
    key = jax.random.fold_in(key, 23)
    return jax.random.uniform(key, (HD,), jnp.float32, 1.5, 2.5)


def block_levels(stream_key, shape, pieces, smallest, largest):
    def one(position, blocks):
        heights = jax.random.uniform(jax.random.fold_in(jax.random.fold_in(stream_key, 6), position), (blocks,), jnp.float32, smallest / len(pieces), largest / len(pieces))
        return jnp.repeat(jnp.exp(heights), shape[position] // blocks).reshape((-1,) + (1,) * (len(shape) - position - 1))

    gain = one(*pieces[0])
    for cut in pieces[1:]:
        gain = gain * one(*cut)
    return gain


def bell_draw(rng, extent, scale, most, shards=(), kind=jnp.bfloat16):
    level = block_levels(rng, extent, shards, -0.22, 0.18) if shards else 1.0
    entries = jax.random.normal(rng, extent, jnp.float32) * scale * level
    return jnp.minimum(jnp.maximum(entries, -most), most).astype(kind)


def setup_inputs(seed: int = 0) -> dict:
    splits = jax.random.split(jax.random.key(seed), 11)
    states = bell_draw(splits[0], (STEPS, L, D), 1.0, 6.0, ((0, 2), (1, 128)), jnp.float32)
    start = bell_draw(splits[1], (L, D), 1.0, 6.0, ((0, 128),), jnp.float32)
    w_qkv = bell_draw(splits[2], (D, 3, D), D ** -0.5, 0.109375, ((0, 16), (2, 8)))
    w_out = bell_draw(splits[3], (D, D), D ** -0.5, 0.109375, ((0, 128),))
    q_gain = draw_q_gain(jax.random.fold_in(splits[10], 71), 0)
    k_gain = draw_k_gain(jax.random.fold_in(splits[10], 71), 0)
    mod_table = bell_draw(splits[6], (TABLE, 3 * D), 0.5, 3.0, (), jnp.float32)
    step_index = jax.random.randint(splits[7], (STEPS,), 0, TABLE).astype(jnp.int32)
    coef_table = jnp.clip(jnp.exp(jax.random.uniform(splits[8], (TABLE,), jnp.float32, math.log(0.1), math.log(1.0))), 0.1, 1.0)
    coef_index = jax.random.randint(splits[9], (STEPS,), 0, TABLE).astype(jnp.int32)
    return dict(states=states, start=start, w_qkv=w_qkv, w_out=w_out, q_gain=q_gain, k_gain=k_gain, mod_table=mod_table, step_index=step_index, coef_table=coef_table, coef_index=coef_index)


def head_norm(values_in, gains):
    middle = lax.optimization_barrier(jnp.mean(values_in, axis=-1, keepdims=True))
    spread = lax.optimization_barrier(jnp.mean((values_in - middle) ** 2, axis=-1, keepdims=True))
    return (values_in - middle) * lax.rsqrt(spread + 1e-06) * gains

def reference(states, start, w_qkv, w_out, q_gain, k_gain, mod_table, step_index, coef_table, coef_index):
    modulation = mod_table[step_index].reshape(STEPS, 3, D)
    coefs = coef_table[coef_index]

    def one_step(packed):
        current, mods = packed
        middle = lax.optimization_barrier(jnp.mean(current, axis=-1, keepdims=True))
        spread = lax.optimization_barrier(jnp.mean((current - middle) ** 2, axis=-1, keepdims=True))
        normed = ((current - middle) * lax.rsqrt(spread + 1e-05) * (1.0 + mods[1]) + mods[0]).astype(jnp.bfloat16)
        projected = jnp.dot(normed, w_qkv.reshape(D, 3 * D), preferred_element_type=jnp.float32).reshape(L, 3, H, HD)
        queries = head_norm(projected[:, 0], q_gain).astype(jnp.bfloat16)
        keys_all = head_norm(projected[:, 1], k_gain).astype(jnp.bfloat16)
        values_all = projected[:, 2].astype(jnp.bfloat16)
        scores = jnp.einsum('qhd,khd->hqk', queries.astype(jnp.float32), keys_all.astype(jnp.float32)) * HD ** (-0.5)
        peak = lax.optimization_barrier(jnp.max(scores, axis=-1, keepdims=True))
        weights = jnp.exp(scores - peak)
        totals = lax.optimization_barrier(jnp.sum(weights, axis=-1))
        mixed = jnp.einsum('hqk,khd->qhd', weights.astype(jnp.bfloat16).astype(jnp.float32), values_all.astype(jnp.float32))
        mixed = mixed / jnp.transpose(totals)[:, :, None]
        attn = mixed.reshape(L, D).astype(jnp.bfloat16)
        return mods[2] * jnp.dot(attn, w_out, preferred_element_type=jnp.float32)
    drifts = lax.map(one_step, (states, modulation))
    return start[None] + jnp.cumsum(coefs[:, None, None] * drifts, axis=0)
```

```python
import jax
import jax.numpy as jnp
from jax import lax
from jax.experimental import pallas as pl
from jax.experimental.pallas import tpu as pltpu
from jax.sharding import Mesh, PartitionSpec as P

HD = 64
BF = jnp.bfloat16
F32 = jnp.float32


def shift_pairs(size, offset):
    return [(i, (i - offset) % size) for i in range(size)]


def head_norm(values_in, gains):
    middle = jnp.mean(values_in, axis=-1, keepdims=True)
    spread = jnp.mean((values_in - middle) ** 2, axis=-1, keepdims=True)
    return (values_in - middle) * lax.rsqrt(spread + 1e-06) * gains


def ring_of_four(block, axis):
    after = lax.ppermute(block, axis, shift_pairs(4, 1))
    before = lax.ppermute(block, axis, shift_pairs(4, 3))
    across = lax.ppermute(block, axis, shift_pairs(4, 2))
    return jnp.stack([block, after, across, before])


def ring_forwarded(block, axis):
    after = lax.ppermute(block, axis, shift_pairs(4, 1))
    before = lax.ppermute(block, axis, shift_pairs(4, 3))
    half = block.shape[0] // 2
    low = lax.ppermute(after[:half], axis, shift_pairs(4, 1))
    high = lax.ppermute(before[half:], axis, shift_pairs(4, 3))
    return [block, after, before, low, high]


def attention_kernel(q_ref, kv_ref, o_ref):
    lane = lax.broadcasted_iota(jnp.int32, (1, 128), 1)
    low = lane < 64
    dims = (((1,), (1,)), ((), ()))

    def head(q_tile, k_tile, v_tile):
        scores = lax.dot_general(q_tile, k_tile, dims, preferred_element_type=F32)
        peak = jnp.max(scores, axis=-1, keepdims=True)
        weights = jnp.exp(scores - peak)
        total = jnp.sum(weights, axis=-1, keepdims=True)
        mixed = jnp.dot(weights.astype(BF), v_tile, preferred_element_type=F32)
        return mixed / total

    pair = q_ref[:, 0:128]
    zero = jnp.zeros_like(pair)
    tile_a, tile_b, tile_c = kv_ref[:, 0:128], kv_ref[:, 128:256], kv_ref[:, 256:384]
    first = head(jnp.where(low, pair, zero), tile_b, tile_c)
    second = head(jnp.where(low, zero, pair), tile_b, tile_c)
    o_ref[:, 0:128] = jnp.where(low, first, second).astype(o_ref.dtype)
    third = head(q_ref[:, 128:256], tile_a, tile_a)
    o_ref[:, 128:192] = third[:, 0:64].astype(o_ref.dtype)


def attention(q, kv):
    rows = q.shape[0]
    vmem = pl.BlockSpec(memory_space=pltpu.VMEM)
    return pl.pallas_call(
        attention_kernel,
        out_shape=jax.ShapeDtypeStruct((rows, 192), BF),
        in_specs=[vmem, vmem],
        out_specs=vmem,
        compiler_params=pltpu.CompilerParams(vmem_limit_bytes=40 * 1024 * 1024),
        cost_estimate=pl.CostEstimate(
            flops=4 * rows * kv.shape[0] * 3 * 128,
            bytes_accessed=kv.size * 2,
            transcendentals=rows * kv.shape[0] * 3,
        ),
    )(q, kv)


def on_device(
    states, start, w_qkv, w_out, q_gain, k_gain, mod_table, step_index, coef_table, coef_index
):
    width = states.shape[2]
    tokens = states.shape[1]
    half = width // 2
    core = lax.axis_index("c")
    at_y = lax.axis_index("y")
    at_x = lax.axis_index("x")
    first_core = core == 0
    swap = [(0, 1), (1, 0)]
    x_pairs = [(i, i ^ 1) for i in range(4)]
    diagonal = [(i, i ^ 5) for i in range(8)]

    w_core = lax.dynamic_slice_in_dim(w_qkv, core * 192, 192, axis=2).reshape(192, 576)
    by_x = ring_of_four(w_core[:96], "x")
    by_y = ring_of_four(w_core[96:], "y")
    pieces = ring_forwarded(by_x, "y") + ring_forwarded(by_y, "x")
    weights = jnp.concatenate([p.reshape(-1, 576) for p in pieces], axis=0)

    w_out_half = lax.dynamic_slice_in_dim(w_out, core * half, half, axis=1)
    w_out_rows = lax.all_gather(w_out_half, ("y", "x"), axis=0, tiled=True)

    own_index = jnp.concatenate([step_index, coef_index])
    other_index = lax.ppermute(own_index, "c", swap)
    first_index = jnp.where(first_core, own_index, other_index)
    second_index = jnp.where(first_core, other_index, own_index)

    row = lax.dynamic_index_in_dim(mod_table, step_index[0], 0, True)
    current = states[0]
    middle = jnp.mean(current, axis=-1, keepdims=True)
    spread = jnp.mean((current - middle) ** 2, axis=-1, keepdims=True)
    normed = (
        (current - middle) * lax.rsqrt(spread + 1e-05) * (1.0 + row[:, width : 2 * width])
        + row[:, :width]
    ).astype(BF)
    blocks = normed.reshape(tokens, 4, 4, 192)
    blocks = lax.dynamic_slice_in_dim(jnp.concatenate([blocks, blocks], axis=1), at_y, 4, axis=1)
    blocks = lax.dynamic_slice_in_dim(jnp.concatenate([blocks, blocks], axis=2), at_x, 4, axis=2)
    order = [0, 1, 3, 2]
    part_x = jnp.concatenate([blocks[:, i : i + 1, :, :96] for i in order], axis=1)
    part_y = jnp.concatenate([blocks[:, :, i : i + 1, 96:] for i in order], axis=2)
    arranged = jnp.concatenate(
        [part_x.reshape(tokens, half), jnp.swapaxes(part_y, 1, 2).reshape(tokens, half)], axis=1
    )
    theirs = lax.ppermute(arranged, "c", swap)
    both = jnp.where(
        first_core, jnp.stack([arranged, theirs]), jnp.stack([theirs, arranged])
    )
    gathered = lax.all_gather(both, "z", axis=0, tiled=False)
    groups = gathered.shape[0]
    rows = groups * tokens

    projected = jnp.dot(
        gathered.reshape(2 * rows, width), weights, preferred_element_type=F32
    ).reshape(groups, 2, tokens, 3, 3, HD)
    projected = jnp.swapaxes(projected, 0, 1).reshape(2, rows, 3, 3, HD)
    queries = (head_norm(projected[:, :, 0], q_gain).astype(BF) * BF(HD**-0.5)).reshape(2, rows, 192)
    keys = head_norm(projected[:, :, 1], k_gain).astype(BF).reshape(2, rows, 192)
    values = projected[:, :, 2].astype(BF).reshape(2, rows, 192)
    queries = jnp.concatenate(
        [queries[..., :128], jnp.zeros_like(queries[..., :64]), queries[..., 128:]], axis=-1
    )
    keys_values = jnp.concatenate(
        [values[..., 128:], keys[..., 128:], keys[..., :128], values[..., :128]], axis=-1
    )

    step = at_x % 2
    first_step = step == 0
    q_kept = jnp.where(first_step, queries[0], queries[1])
    q_given = jnp.where(first_step, queries[1], queries[0])
    q_got = lax.ppermute(q_given, "x", x_pairs)
    outgoing = jnp.broadcast_to(keys_values[None], (8, 2, rows, 384)).reshape(16, rows, 384)
    incoming = lax.all_to_all(outgoing, ("y", "x"), 0, 0, tiled=True)
    attn = attention(jnp.concatenate([q_kept, q_got], axis=0), incoming.reshape(16 * rows, 384))

    mine, partners = attn[:rows], attn[rows:]
    mine_core = lax.ppermute(mine, "c", swap)
    here = lax.ppermute(partners, "x", x_pairs)
    here_core = lax.ppermute(partners, ("c", "x"), diagonal)

    def heads_in_order(own, other):
        return jnp.where(
            first_core,
            jnp.concatenate([own, other], axis=1),
            jnp.concatenate([other, own], axis=1),
        )

    this_step, that_step = heads_in_order(mine, mine_core), heads_in_order(here, here_core)
    features = jnp.where(
        first_step, jnp.stack([this_step, that_step]), jnp.stack([that_step, this_step])
    )
    features = jnp.swapaxes(features.reshape(2, groups, tokens, 384), 0, 1)
    share = jnp.dot(
        features.reshape(2 * rows, 384), w_out_rows, preferred_element_type=F32
    ).astype(BF)
    arrived = lax.all_to_all(share.reshape(groups, 2 * tokens, half), "z", 0, 0, tiled=True)
    mixed = jnp.sum(arrived.astype(F32), axis=0).reshape(2, tokens, half)

    def weighted(index, drift):
        gate = lax.dynamic_slice(mod_table, (index[0], 2 * width + core * half), (1, half))
        return coef_table[index[1]] * (gate * drift)

    first = weighted(first_index, mixed[0])
    second = first + weighted(second_index, mixed[1])
    kept = jnp.where(first_core, first, second)
    given = jnp.where(first_core, second, first)
    got = lax.ppermute(given, "c", swap)
    moved = jnp.where(
        first_core,
        jnp.concatenate([kept, got], axis=1),
        jnp.concatenate([got, kept], axis=1),
    )
    return (start + moved)[None]


def solution(mesh):
    grid = Mesh(mesh.devices.reshape(2, 8, 4, 4), ("c", "z", "y", "x"))
    tokens = ("z", "y", "x")
    in_specs = (
        P("c", tokens, None),
        P(tokens, None),
        P(("y", "x"), None, "z"),
        P(tokens, None),
        P(),
        P(),
        P(),
        P("c"),
        P(),
        P("c"),
    )
    return jax.shard_map(
        on_device, mesh=grid, in_specs=in_specs, out_specs=P("c", tokens, None), check_vma=False
    )
```

```python
import jax
import jax.numpy as jnp
from jax import lax
from jax.experimental import pallas as pl
from jax.experimental.pallas import tpu as pltpu
from jax.sharding import Mesh, PartitionSpec as P

HD = 64
BF = jnp.bfloat16
F32 = jnp.float32
SMALL = ("c", "y0", "x0")
PLANE = ("y1", "y0", "x1", "x0")
VMEM = pl.BlockSpec(memory_space=pltpu.VMEM)
SMEM = pl.BlockSpec(memory_space=pltpu.SMEM)
SWAP = [(0, 1), (1, 0)]


def plane_pairs(dy, dx):
    return [
        (y * 4 + x, (y - dy) % 4 * 4 + (x - dx) % 4) for y in range(4) for x in range(4)
    ]


def small_pairs(target):
    pairs = []
    for core in range(2):
        for y in range(2):
            for x in range(2):
                to_core, to_y, to_x = target(core, y, x)
                pairs.append((core * 4 + y * 2 + x, to_core * 4 + to_y * 2 + to_x))
    return pairs


def ring_of_four(block, dy, dx):
    after = lax.ppermute(block, PLANE, plane_pairs(dy, dx))
    before = lax.ppermute(block, PLANE, plane_pairs(-dy, -dx))
    across = lax.ppermute(block, PLANE, plane_pairs(2 * dy, 2 * dx))
    return jnp.stack([block, after, across, before])


def ring_forwarded(block, dy, dx):
    after = lax.ppermute(block, PLANE, plane_pairs(dy, dx))
    before = lax.ppermute(block, PLANE, plane_pairs(-dy, -dx))
    low = lax.ppermute(after[:2], PLANE, plane_pairs(dy, dx))
    high = lax.ppermute(before[2:], PLANE, plane_pairs(-dy, -dx))
    return [block, after, before, low, high]


def low_lanes():
    return lax.broadcasted_iota(jnp.int32, (1, 128), 1) < 64


def roll64(tile):
    return pltpu.roll(tile, 64, 1)


def normalize_pair(tile, gains, low):
    def per_head(values):
        first = jnp.sum(jnp.where(low, values, 0.0), axis=1, keepdims=True)
        second = jnp.sum(jnp.where(low, 0.0, values), axis=1, keepdims=True)
        return jnp.where(low, first, second) * (1.0 / HD)

    centered = tile - per_head(tile)
    return centered * lax.rsqrt(per_head(centered * centered) + 1e-06) * gains


def project_kernel(
    core_ref, own_ref, other_ref, gain_ref, *refs
):
    pieces, (kv_ref, q_ref), acc = refs[:10], refs[10:12], refs[12]
    low = low_lanes()
    first_core = core_ref[0] == 0

    def term(i):
        if i % 4 == 3:
            low_half, high_half = pieces[i // 4 * 5 + 3], pieces[i // 4 * 5 + 4]
            block = jnp.concatenate([low_half[...], high_half[...]], axis=0)
        else:
            block = pieces[i // 4 * 5 + i % 4][...]
        columns = pl.ds(i * 384, 384)
        for r, ref in enumerate((own_ref, other_ref)):
            value = jnp.dot(ref[:, columns], block, preferred_element_type=F32)
            if i == 0:
                acc[r] = value
            else:
                acc[r] += value

    for i in range(8):
        term(i)

    def of_step(step, columns):
        own, other = acc[0, :, columns], acc[1, :, columns]
        return jnp.where(first_core, own, other) if step == 0 else jnp.where(first_core, other, own)

    q_gain, k_gain = gain_ref[0:1, :], gain_ref[1:2, :]
    for step in range(2):
        tiles = []
        for t in range(3):
            raw = of_step(step, slice(t * 128, t * 128 + 128))
            normed = normalize_pair(raw, k_gain, low)
            tiles.append(jnp.where(first_core, normed, raw))
        lo, hi = slice(0, 64), slice(64, 128)
        for half, (t, m) in enumerate(
            (
                (tiles[0], jnp.where(low, tiles[1][lo], roll64(tiles[1][hi]))),
                (tiles[2], jnp.where(low, roll64(tiles[1][lo]), tiles[1][hi])),
            )
        ):
            kv_ref[half, step, :, 0:128] = t[lo].astype(BF)
            kv_ref[half, step, :, 128:256] = t[hi].astype(BF)
            kv_ref[half, step, :, 256:384] = m.astype(BF)
        pair = normalize_pair(of_step(step, slice(384, 512)), q_gain, low).astype(BF)
        last = of_step(step, slice(512, 576))
        last = jnp.concatenate([last, last], axis=1)
        last = normalize_pair(last, q_gain, low).astype(BF)
        factor = jnp.asarray(HD**-0.5, BF)
        q_ref[step, :, 0:128] = pair[lo] * factor
        q_ref[step, :, 128:256] = pair[hi] * factor
        q_ref[step, :, 256:384] = jnp.where(low, last[lo], last[hi]) * factor


def project(core, own, other, gains, pieces):
    rows = own.shape[0]
    return pl.pallas_call(
        project_kernel,
        out_shape=(
            jax.ShapeDtypeStruct((2, 2, 64, 384), BF),
            jax.ShapeDtypeStruct((2, 64, 384), BF),
        ),
        in_specs=[SMEM] + [VMEM] * 13,
        out_specs=(VMEM, VMEM),
        scratch_shapes=[pltpu.VMEM((2, rows, 576), F32)],
        compiler_params=pltpu.CompilerParams(vmem_limit_bytes=40 * 1024 * 1024),
        cost_estimate=pl.CostEstimate(
            flops=4 * rows * 3072 * 576, bytes_accessed=3072 * 576 * 2, transcendentals=0
        ),
    )(core, own, other, gains, *pieces)


def attention_kernel(core_ref, q0_ref, q1_ref, mine_ref, theirs_ref, o0_ref, o1_ref):
    low = low_lanes()
    first_core = core_ref[0] == 0
    dims = (((1,), (1,)), ((), ()))

    def key(t):
        a, b = mine_ref[:, t * 128 : t * 128 + 128], theirs_ref[:, t * 128 : t * 128 + 128]
        return jnp.where(first_core, a, b)

    def value(t):
        a, b = mine_ref[:, t * 128 : t * 128 + 128], theirs_ref[:, t * 128 : t * 128 + 128]
        return jnp.where(first_core, b, a)

    def head(q_a, q_b, k_a, k_b, v_a, v_b, shifted):
        s_a = lax.dot_general(q_a, k_a, dims, preferred_element_type=F32)
        s_b = lax.dot_general(q_b, k_b, dims, preferred_element_type=F32)
        peak = jnp.maximum(
            jnp.max(s_a, axis=-1, keepdims=True), jnp.max(s_b, axis=-1, keepdims=True)
        )
        w_a, w_b = jnp.exp(s_a - peak), jnp.exp(s_b - peak)
        total = jnp.sum(w_a, axis=-1, keepdims=True) + jnp.sum(w_b, axis=-1, keepdims=True)
        m_a = jnp.dot(w_a.astype(BF), v_a, preferred_element_type=F32)
        m_b = jnp.dot(w_b.astype(BF), v_b, preferred_element_type=F32)
        return (m_a + (roll64(m_b) if shifted else m_b)) / total

    q_pair = jnp.concatenate(
        [q0_ref[:, 0:128], q1_ref[:, 0:128], q0_ref[:, 128:256], q1_ref[:, 128:256]], axis=0
    )
    zero = jnp.zeros_like(q_pair)
    q_first, q_second = jnp.where(low, q_pair, zero), jnp.where(low, zero, q_pair)
    k_lo, k_hi, v_lo, v_hi = key(0), key(1), value(0), value(1)
    first = head(q_first, q_first, k_lo, k_hi, v_lo, v_hi, False)
    second = head(q_second, q_second, k_lo, k_hi, v_lo, v_hi, False)
    both = jnp.where(low, first, second).astype(BF)
    last = jnp.concatenate([q0_ref[:, 256:384], q1_ref[:, 256:384]], axis=0).astype(F32)
    turned = roll64(last)
    q_low = jnp.where(low, jnp.concatenate([last, turned], axis=0), 0.0).astype(BF)
    q_high = jnp.where(low, 0.0, jnp.concatenate([turned, last], axis=0)).astype(BF)
    third = head(q_low, q_high, key(2), key(2), value(2), value(2), True)
    for i, ref in enumerate((o0_ref, o1_ref)):
        lo, hi = slice(64 * i, 64 * i + 64), slice(128 + 64 * i, 192 + 64 * i)
        ref[:, 0:128] = both[lo]
        ref[:, 128:256] = both[hi]
        ref[:, 256:384] = jnp.where(low, third[lo], roll64(third[hi])).astype(BF)


def attention(core, q0, q1, mine, theirs):
    keys = 2 * mine.shape[0]
    return pl.pallas_call(
        attention_kernel,
        out_shape=(jax.ShapeDtypeStruct((64, 384), BF),) * 2,
        in_specs=[SMEM] + [VMEM] * 4,
        out_specs=(VMEM, VMEM),
        compiler_params=pltpu.CompilerParams(vmem_limit_bytes=40 * 1024 * 1024),
        cost_estimate=pl.CostEstimate(
            flops=4 * 256 * keys * 3 * 128,
            bytes_accessed=mine.size * 4,
            transcendentals=256 * keys * 3,
        ),
    )(core, q0, q1, mine, theirs)


def output_kernel(bits_ref, p00_ref, p01_ref, p10_ref, p11_ref, w_ref, o_ref):
    low = low_lanes()
    first_core, first_step = bits_ref[0] == 0, bits_ref[1] == 0

    def half_of(step, half, t):
        columns = slice(t * 128, t * 128 + 128)

        def of(near, far):
            a, b = near[:, columns].astype(F32), far[:, columns].astype(F32)
            return jnp.where(first_core, a, b) if half == 0 else jnp.where(first_core, b, a)

        this, that = of(p00_ref, p01_ref), of(p10_ref, p11_ref)
        return jnp.where(first_step, this, that) if step == 0 else jnp.where(first_step, that, this)

    rows = []
    for step in range(2):
        near = [half_of(step, 0, t) for t in range(3)]
        far = [half_of(step, 1, t) for t in range(3)]
        for part in range(2):
            if part == 0:
                middle = jnp.where(low, near[2], roll64(far[2]))
            else:
                middle = jnp.where(low, roll64(near[2]), far[2])
            rows.append(jnp.concatenate([near[part], middle, far[part]], axis=1).astype(BF))
    features = jnp.concatenate(rows, axis=0)
    for column in range(0, w_ref.shape[1], 512):
        columns = slice(column, column + 512)
        result = jnp.dot(features, w_ref[:, columns], preferred_element_type=F32).astype(BF)
        for step in range(2):
            for z in range(8):
                at = step * 128 + z * 16
                o_ref[z, step * 16 : step * 16 + 16, columns] = result[at : at + 16]


def output_projection(bits, parts, w_rows):
    width = w_rows.shape[1]
    return pl.pallas_call(
        output_kernel,
        out_shape=jax.ShapeDtypeStruct((8, 32, width), BF),
        in_specs=[SMEM] + [VMEM] * 5,
        out_specs=VMEM,
        compiler_params=pltpu.CompilerParams(vmem_limit_bytes=40 * 1024 * 1024),
        cost_estimate=pl.CostEstimate(
            flops=2 * 256 * 384 * width, bytes_accessed=w_rows.size * 2, transcendentals=0
        ),
    )(bits, *parts, w_rows)


def on_device(
    states, start, w_qkv, w_out, q_gain, k_gain, mod_table, step_index, coef_table, coef_index
):
    width = states.shape[2]
    tokens = states.shape[1]
    half = width // 2
    core = lax.axis_index("c")
    at_y = lax.axis_index(("y1", "y0"))
    at_x = lax.axis_index(("x1", "x0"))
    first_core = core == 0
    core_bit = core.astype(jnp.int32).reshape(1)
    bits = jnp.stack([core, lax.axis_index("x0")]).astype(jnp.int32)

    row = lax.dynamic_index_in_dim(mod_table, step_index[0], 0, True)
    current = states[0]
    middle = jnp.mean(current, axis=-1, keepdims=True)
    spread = jnp.mean((current - middle) ** 2, axis=-1, keepdims=True)
    normed = (
        (current - middle) * lax.rsqrt(spread + 1e-05) * (1.0 + row[:, width : 2 * width])
        + row[:, :width]
    ).astype(BF)
    blocks = normed.reshape(tokens, 4, 4, 192)
    blocks = lax.dynamic_slice_in_dim(jnp.concatenate([blocks, blocks], axis=1), at_y, 4, axis=1)
    blocks = lax.dynamic_slice_in_dim(jnp.concatenate([blocks, blocks], axis=2), at_x, 4, axis=2)
    order = [0, 1, 3, 2]
    part_x = jnp.concatenate([blocks[:, i : i + 1, :, :96] for i in order], axis=1)
    part_y = jnp.concatenate([blocks[:, :, i : i + 1, 96:] for i in order], axis=2)
    arranged = jnp.concatenate(
        [part_x.reshape(tokens, half), jnp.swapaxes(part_y, 1, 2).reshape(tokens, half)], axis=1
    )
    own = lax.all_to_all(
        jnp.broadcast_to(arranged[None], (8, tokens, width)), "z", 0, 0, tiled=True
    ).reshape(8 * tokens, width)
    other = lax.ppermute(own, "c", SWAP)

    w_kv = jnp.where(first_core, w_qkv[:, 1], w_qkv[:, 2])
    w_q = w_qkv[:, 0]
    w_q = jnp.where(
        first_core, w_q[:, :192], jnp.concatenate([w_q[:, 256:], w_q[:, 192:256]], axis=1)
    )
    w_core = jnp.concatenate([w_kv, w_q], axis=1)
    by_x = ring_of_four(w_core[:96], 0, 1)
    by_y = ring_of_four(w_core[96:], 1, 0)
    pieces = ring_forwarded(by_x, 1, 0) + ring_forwarded(by_y, 0, 1)
    pieces = [p.reshape(-1, 576) for p in pieces]

    gains = jnp.stack([jnp.tile(q_gain, 2), jnp.tile(k_gain, 2)])
    keys_values, queries = project(core_bit, own, other, gains, pieces)

    outgoing = jnp.broadcast_to(keys_values[None, :, None], (2, 2, 2, 2, 64, 384))
    mine = lax.all_to_all(outgoing.reshape(16, 64, 384), PLANE, 0, 0, tiled=True)
    mine = mine.reshape(1024, 384)
    theirs = lax.ppermute(mine, "c", SWAP)
    first_x = lax.axis_index("x0") == 0
    this_q = jnp.where(first_x, queries[0], queries[1])
    that_q = jnp.where(first_x, queries[1], queries[0])
    q0 = lax.ppermute(this_q, SMALL, small_pairs(lambda c, y, x: (y, c, x)))
    q1 = lax.ppermute(that_q, SMALL, small_pairs(lambda c, y, x: (y, c, 1 - x)))

    w_half = lax.dynamic_slice_in_dim(w_out, core * half, half, axis=1)
    w_half, mine = lax.optimization_barrier((w_half, mine))
    w_rows = lax.all_to_all(
        jnp.broadcast_to(w_half[None], (16,) + w_half.shape), PLANE, 0, 0, tiled=True
    ).reshape(384, half)

    o0, o1 = attention(core_bit, q0, q1, mine, theirs)

    parts = [
        lax.ppermute(o, SMALL, small_pairs(lambda c, y, x, k=k, m=m: (y ^ m, c, x ^ k)))
        for k, o in enumerate((o0, o1))
        for m in range(2)
    ]
    share = output_projection(bits, parts, w_rows)
    arrived = lax.all_to_all(share, "z", 0, 0, tiled=True)
    mixed = jnp.sum(arrived.astype(F32), axis=0).reshape(2, tokens, half)

    own_index = jnp.concatenate([step_index, coef_index])
    other_index = lax.ppermute(own_index, "c", SWAP)

    def weighted(index, drift):
        gate = lax.dynamic_slice(mod_table, (index[0], 2 * width + core * half), (1, half))
        return coef_table[index[1]] * (gate * drift)

    first = weighted(jnp.where(first_core, own_index, other_index), mixed[0])
    second = first + weighted(jnp.where(first_core, other_index, own_index), mixed[1])
    kept = jnp.where(first_core, first, second)
    given = jnp.where(first_core, second, first)
    got = lax.ppermute(given, "c", SWAP)
    moved = jnp.where(
        first_core,
        jnp.concatenate([kept, got], axis=1),
        jnp.concatenate([got, kept], axis=1),
    )
    return (start + moved)[None]


def solution(mesh):
    grid = Mesh(mesh.devices.reshape(2, 8, 2, 2, 2, 2), ("c", "z") + PLANE)
    tokens = ("z",) + PLANE
    in_specs = (
        P("c", tokens, None),
        P(tokens, None),
        P(PLANE, None, "z"),
        P(tokens, None),
        P(),
        P(),
        P(),
        P("c"),
        P(),
        P("c"),
    )
    return jax.shard_map(
        on_device, mesh=grid, in_specs=in_specs, out_specs=P("c", tokens, None), check_vma=False
    )
```
